32 devices in a mesh: parts: 2 (over x), leaf: 16 (over z, y, core).
Axes of the slice: x: 2, y: 2, z: 4, core: 2. Of those that a mesh axis runs over, the one named last changes fastest.
Arguments:
- points: float32 [3, 65536], P(None, ('parts', 'leaf')), parts along dimension 1, may hold values from 0 to 18
- charges: bfloat16 [16, 65536], P(None, ('parts', 'leaf')), parts along dimension 1, may hold values from -6 to 6
- near_list: int32 [256, 12], P(('parts', 'leaf')), parts along dimension 0, may hold values from -1 to 127, as said below
- basis: bfloat16 [256, 64, 256], P(('parts', 'leaf')), parts along dimension 0, may hold values from -0.75 to 0.75
- leaf_transfer: bfloat16 [256, 64, 64], P(('parts', 'leaf')), parts along dimension 0, may hold values from -0.25 to 0.25
- cluster_transfer: bfloat16 [32, 64, 64], P(('parts', 'leaf')), parts along dimension 0, may hold values from -0.25 to 0.25
- couple_one: bfloat16 [32, 6, 64, 64], P(('parts', 'leaf')), parts along dimension 0, may hold values from -0.3125 to 0.3125
- far_list: int32 [32, 6], P(('parts', 'leaf')), parts along dimension 0, may hold values from -1 to 15, as said below
- couple_two: bfloat16 [4, 2, 64, 64], P('parts'), parts along dimension 0, may hold values from -0.5 to 0.5
Outputs:
- potential: float32 [16, 65536], P(None, ('parts', 'leaf')), parts along dimension 1
The draws below stay inside these ranges and needn't reach their ends.
There are 2 independent parts, one for each index of `parts`. The reference program is written for one: setup_inputs(seed, part) draws one part's arguments, and reference() takes and returns one part's arrays. A program takes and returns all parts, laid end to end along the dimension named above; each array names one. Nothing has to cross between parts.
Inputs may be any that keep to these rules, and one draw needn't show every extreme that they name: `near_list`: row i holds distinct leaves j with |j - i| <= 8, the used entries first and -1 after them; every row has at least one used entry; some row is full. `far_list`: slot s of row c holds -1 or c plus the s-th of the offsets -4 to -2 and 2 to 4 in increasing order.
All inputs are finite; a program needn't handle non-finite values.
Results may differ from the reference program's by a relative error of at most 0.0029.
Values may be sent and summed in bfloat16 or wider, within the bound.
A program may use at most 64 MiB of HBM per device.

```python
import math
import jax
import jax.numpy as jnp
from jax import lax

LEAF_SIZE = 256
RANK = 64
VECTORS = 16
LEAF_DEV = 8
NEAR_MOST = 12
FAR_REACH = 4
FAR_SLOTS = 6
GROUP = 8
LEAVES = 128
PANELS = 32768
CLUSTERS1 = 16
CLUSTERS2 = 2


def draw_points(key, part):
    key = jax.random.fold_in(key, 1)
    spread = jax.random.uniform(key, (3, PANELS), jnp.float32)
    leaf_place = (jnp.arange(PANELS) // LEAF_SIZE).astype(jnp.float32) / LEAF_DEV
    return jnp.stack([leaf_place + spread[0], spread[1], spread[2]]).astype(jnp.float32)


def draw_near_list(key, part):
    key = jax.random.fold_in(key, 7)
    first, second, third, fourth, fifth = jax.random.split(key, 5)
    width = 2 * LEAF_DEV + 1
    leaves = jnp.arange(LEAVES, dtype=jnp.int32)
    offsets = jnp.arange(width, dtype=jnp.int32) - LEAF_DEV
    candidate = leaves[:, None] + offsets[None, :]
    inside = (candidate >= 0) & (candidate < LEAVES)
    scores = jax.random.randint(first, (LEAVES, width), 0, 1 << 20) * (width + 1) + jnp.arange(width, dtype=jnp.int32)[None, :]
    scores = jnp.where(inside, scores, (1 << 30) + jnp.arange(width, dtype=jnp.int32)[None, :])
    order = jnp.argsort(scores, axis=1, stable=True)
    picked = jnp.take_along_axis(candidate, order[:, :NEAR_MOST], axis=1)
    available = jnp.sum(inside.astype(jnp.int32), axis=1)
    busy = jax.random.randint(second, (LEAVES // LEAF_DEV,), 0, 4) == 0
    busy_leaf = jnp.repeat(busy, LEAF_DEV)
    light = jax.random.randint(third, (LEAVES,), 1, NEAR_MOST // 3 + 1)
    heavy = jax.random.randint(fourth, (LEAVES,), NEAR_MOST // 2, NEAR_MOST + 1)
    count = jnp.where(busy_leaf, heavy, light)
    chosen = jax.random.randint(fifth, (), LEAF_DEV, LEAVES - LEAF_DEV)
    count = jnp.where(leaves == chosen, NEAR_MOST, count)
    count = jnp.minimum(count, available)
    slots = jnp.arange(NEAR_MOST, dtype=jnp.int32)
    return jnp.where(slots[None, :] < count[:, None], picked, -1).astype(jnp.int32)


def draw_far_list(key, part):
    key = jax.random.fold_in(key, 11)
    offsets = jnp.concatenate([jnp.arange(-FAR_REACH, -1), jnp.arange(2, FAR_REACH + 1)]).astype(jnp.int32)
    clusters = jnp.arange(CLUSTERS1, dtype=jnp.int32)
    candidate = clusters[:, None] + offsets[None, :]
    keep = jax.random.randint(key, (CLUSTERS1, FAR_SLOTS), 0, 4) > 0
    keep = keep & (candidate >= 0) & (candidate < CLUSTERS1)
    return jnp.where(keep, candidate, -1).astype(jnp.int32)


def block_scale(key, shape, shards, low, top_value):
    def one(dim, parts):
        draws = jax.random.uniform(jax.random.fold_in(jax.random.fold_in(key, 6), dim), (parts,), jnp.float32, low / len(shards), top_value / len(shards))
        return jnp.repeat(jnp.exp(draws), shape[dim] // parts).reshape((-1,) + (1,) * (len(shape) - dim - 1))

    gain = one(*shards[0])
    for cut in shards[1:]:
        gain = gain * one(*cut)
    return gain


def scatter_about(key, dims, scale, limit, cuts=(), held_as=jnp.bfloat16):
    loudness = block_scale(key, dims, cuts, -0.22, 0.18) if cuts else 1.0
    values = jax.random.normal(key, dims, jnp.float32) * scale * loudness
    return jnp.minimum(jnp.maximum(values, -limit), limit).astype(held_as)


def setup_inputs(seed: int = 0, part: int = 0) -> dict:
    seeds = jax.random.split(jax.random.key(seed), 10)
    part_keys = jax.random.split(jax.random.fold_in(seeds[9], part), 10)
    points = draw_points(jax.random.fold_in(jax.random.fold_in(seeds[9], part), 71), part)
    charges = scatter_about(part_keys[1], (VECTORS, PANELS), 1.0, 6.0, ((1, 16),))
    near_list = draw_near_list(jax.random.fold_in(jax.random.fold_in(seeds[9], part), 71), part)
    basis = scatter_about(part_keys[3], (LEAVES, RANK, LEAF_SIZE), (LEAF_SIZE // 4) ** -0.5, 0.75, ((0, 16),))
    leaf_transfer = scatter_about(part_keys[4], (LEAVES, RANK, RANK), (RANK * LEAF_DEV) ** -0.5, 0.25, ((0, 16),))
    cluster_transfer = scatter_about(part_keys[5], (CLUSTERS1, RANK, RANK), (RANK * GROUP) ** -0.5, 0.25, ((0, 16),))
    couple_one = scatter_about(part_keys[6], (CLUSTERS1, FAR_SLOTS, RANK, RANK), (RANK * FAR_SLOTS) ** -0.5, 0.3125, ((0, 16),))
    far_list = draw_far_list(jax.random.fold_in(jax.random.fold_in(seeds[9], part), 71), part)
    couple_two = scatter_about(part_keys[8], (CLUSTERS2, CLUSTERS2, RANK, RANK), (RANK * CLUSTERS2) ** -0.5, 0.5)
    return dict(points=points, charges=charges, near_list=near_list, basis=basis, leaf_transfer=leaf_transfer, cluster_transfer=cluster_transfer, couple_one=couple_one, far_list=far_list, couple_two=couple_two)


inv_four_pi = 1.0 / (4.0 * math.pi)
soften = 0.01

def near_kernel(target, source, usable):
    square = jnp.square(target[0][None, :, None] - source[0][:, None, :])
    square = square + jnp.square(target[1][None, :, None] - source[1][:, None, :])
    square = square + jnp.square(target[2][None, :, None] - source[2][:, None, :])
    return usable[:, None, None] * inv_four_pi / jnp.sqrt(square + soften)

def reference(points, charges, near_list, basis, leaf_transfer, cluster_transfer, couple_one, far_list, couple_two):
    high = lax.Precision.HIGHEST
    grid_points = points.reshape(3, LEAVES, LEAF_SIZE)
    grid_charges = charges.reshape(VECTORS, LEAVES, LEAF_SIZE)
    usable = (near_list >= 0).astype(jnp.float32)
    safe = jnp.maximum(near_list, 0).astype(jnp.int32)

    def one_leaf(packed):
        target, index, valid = packed
        source = grid_points[:, index, :]
        source_charge = grid_charges[:, index, :]
        kernel = near_kernel(target, source, valid).astype(jnp.bfloat16)
        return jnp.einsum('npq,vnq->vp', kernel.astype(jnp.float32), source_charge.astype(jnp.float32), precision=high)
    near = lax.map(one_leaf, (jnp.moveaxis(grid_points, 1, 0), safe, usable))
    near = jnp.moveaxis(near, 0, 1).reshape(VECTORS, PANELS)
    leaf_moment = jnp.einsum('lrp,vlp->lrv', basis.astype(jnp.float32), grid_charges.astype(jnp.float32), precision=high)
    transfer = leaf_transfer.astype(jnp.float32).reshape(CLUSTERS1, LEAF_DEV, RANK, RANK)
    moment_one = jnp.einsum('ckab,ckbv->cav', transfer, leaf_moment.reshape(CLUSTERS1, LEAF_DEV, RANK, VECTORS), precision=high)
    upper = cluster_transfer.astype(jnp.float32)
    terms = jnp.einsum('cab,cbv->cav', upper, moment_one, precision=high)
    moment_two = terms.reshape(CLUSTERS2, GROUP, RANK, VECTORS).sum(axis=1)
    groups = jnp.arange(CLUSTERS2, dtype=jnp.int32)
    pair_mask = (groups[:, None] != groups[None, :]).astype(jnp.float32)
    local_two = jnp.einsum('ghab,gh,hbv->gav', couple_two.astype(jnp.float32), pair_mask, moment_two, precision=high)
    far_valid = (far_list >= 0).astype(jnp.float32)
    far_safe = jnp.maximum(far_list, 0).astype(jnp.int32)
    remote = moment_one[far_safe] * far_valid[:, :, None, None]
    local_one = jnp.einsum('csab,csbv->cav', couple_one.astype(jnp.float32), remote, precision=high)
    local_one = local_one + jnp.einsum('cba,cbv->cav', upper, jnp.repeat(local_two, GROUP, axis=0), precision=high)
    local_leaf = jnp.einsum('ckba,cbv->ckav', transfer, local_one, precision=high).reshape(LEAVES, RANK, VECTORS)
    local_leaf = local_leaf.astype(jnp.bfloat16)
    far = jnp.einsum('lrv,lrp->vlp', local_leaf.astype(jnp.float32), basis.astype(jnp.float32), precision=high)
    return near + far.reshape(VECTORS, PANELS)
```

```python
import functools
import math

import jax
import jax.numpy as jnp
from jax import lax
from jax.experimental import pallas as pl
from jax.experimental.pallas import tpu as pltpu
from jax.sharding import PartitionSpec as P

FAR_REACH = 4
OFFSETS = tuple(range(-FAR_REACH, -1)) + tuple(range(2, FAR_REACH + 1))
SCALE = 4.0 * math.pi
SOFT = 0.01 * SCALE * SCALE
STACK = 4
ROWS = 32
NN = (((1,), (0,)), ((), ()))
NT = (((1,), (1,)), ((), ()))
MESH = pl.DeviceIdType.MESH
f32 = jnp.float32
bf16 = jnp.bfloat16


def dot(a, b, dims):
    return lax.dot_general(a, b, dims, preferred_element_type=f32)


def fine_dot(a, b, dims):
    high = a.astype(bf16)
    low = (a - high.astype(f32)).astype(bf16)
    both = dot(jnp.concatenate([high, low], axis=0), b, dims)
    return both[: a.shape[0]] + both[a.shape[0] :]


def pieces(x):
    first = x.astype(bf16).astype(f32)
    rest = x - first
    second = rest.astype(bf16).astype(f32)
    third = (rest - second).astype(bf16).astype(f32)
    return first, second, third


def body(
    n,
    expanded,
    points,
    charges,
    near_list,
    basis,
    leaf_transfer,
    cluster_transfer,
    couple_one,
    far_list,
    couple_two,
    out,
    halo_points,
    halo_charges,
    source_charges,
    source,
    target,
    rows,
    moments,
    halo_send,
    halo_recv,
    moment_send,
    moment_recv,
):
    leaves, rank, width = basis.shape
    vectors = charges.shape[0]
    groups = couple_two.shape[0]
    group_size = n // groups
    slots = near_list.shape[1]
    me = lax.axis_index("leaf")

    barrier = pltpu.get_barrier_semaphore()

    def greet(d, carry):
        pl.semaphore_signal(
            barrier, inc=1, device_id={"leaf": lax.rem(me + d, n)}, device_id_type=MESH
        )
        return carry

    lax.fori_loop(1, n, greet, 0)

    moment_one = jnp.zeros((vectors, rank), f32)
    for k in range(leaves):
        own = charges[:, k * width : (k + 1) * width]
        source_charges[leaves + k] = own
        leaf_moment = dot(own, basis[k], NT)
        moment_one = moment_one + fine_dot(leaf_moment, leaf_transfer[k], NT)
    own_term = fine_dot(moment_one, cluster_transfer[0], NT)
    moments[me] = jnp.concatenate([moment_one, own_term], axis=1)

    pl.semaphore_wait(barrier, n - 1)

    def halo_copies(side):
        to = me + 1 if side == 0 else me - 1
        return [
            pltpu.make_async_remote_copy(
                src_ref=src,
                dst_ref=dst.at[side],
                send_sem=halo_send.at[side, m],
                recv_sem=halo_recv.at[side, m],
                device_id={"leaf": to},
                device_id_type=MESH,
            )
            for m, (src, dst) in enumerate(
                ((points, halo_points), (charges, halo_charges))
            )
        ]

    has_left, has_right = me > 0, me < n - 1

    @pl.when(has_right)
    def _():
        for copy in halo_copies(0):
            copy.start()

    @pl.when(has_left)
    def _():
        for copy in halo_copies(1):
            copy.start()

    def moment_copy(d):
        return pltpu.make_async_remote_copy(
            src_ref=moments.at[me],
            dst_ref=moments.at[me],
            send_sem=moment_send.at[d],
            recv_sem=moment_recv.at[d],
            device_id={"leaf": lax.rem(me + d, n)},
            device_id_type=MESH,
        )

    def send_moments(d, carry):
        moment_copy(d).start()
        return carry

    lax.fori_loop(1, n, send_moments, 0)

    @pl.when(jnp.logical_not(has_left))
    def _():
        halo_points[0] = jnp.zeros(halo_points.shape[1:], f32)
        halo_charges[0] = jnp.zeros(halo_charges.shape[1:], bf16)

    @pl.when(jnp.logical_not(has_right))
    def _():
        halo_points[1] = jnp.zeros(halo_points.shape[1:], f32)
        halo_charges[1] = jnp.zeros(halo_charges.shape[1:], bf16)

    own_points = points[...]
    if expanded:
        low = jnp.min(own_points, axis=1, keepdims=True)
        high = jnp.max(own_points, axis=1, keepdims=True)
        centre = (low + high) * 0.5
        rows[...] = jnp.zeros(rows.shape, f32)

        def put_rows(x, is_source):
            x = (x - centre) * SCALE
            square = jnp.sum(x * x, axis=0, keepdims=True)
            one = jnp.ones(square.shape, f32)
            if is_source:
                a, b, c = pieces(x)
                order = (a, a, a, b, b, c)
                ends = (*pieces(square), one, one, one)
            else:
                a, b, c = pieces(x * -2.0)
                order = (a, b, c, a, b, a)
                ends = (one, one, one, *pieces(square + SOFT))
            for m, block in enumerate(order):
                rows[3 * m : 3 * m + 3] = block
            for m, row in enumerate(ends):
                rows[18 + m : 19 + m] = row

        def put_sources(x, first):
            put_rows(x, True)
            for k in range(leaves):
                block = rows[:, k * width : (k + 1) * width]
                source[first + k] = jnp.transpose(block).astype(bf16)

        put_rows(own_points, False)
        for k in range(leaves):
            target[k] = rows[:, k * width : (k + 1) * width].astype(bf16)
    else:

        def put_sources(x, first):
            x = x * SCALE
            for k in range(leaves):
                source[first + k, 0:3] = x[:, k * width : (k + 1) * width]

    put_sources(own_points, leaves)

    @pl.when(has_left)
    def _():
        for copy in halo_copies(0):
            copy.wait_recv()

    @pl.when(has_right)
    def _():
        for copy in halo_copies(1):
            copy.wait_recv()

    for side in range(2):
        put_sources(halo_points[side], 2 * leaves * side)
        for k in range(leaves):
            source_charges[2 * leaves * side + k] = halo_charges[
                side, :, k * width : (k + 1) * width
            ]

    first_leaf = (me - 1) * leaves

    def one_leaf(i, carry):
        def slot_of(s):
            j = near_list[i, s]
            used = j >= 0
            j = jnp.clip(jnp.where(used, j - first_leaf, leaves), 0, 3 * leaves - 1)
            return j, source_charges[j] * used.astype(f32).astype(bf16)

        near = jnp.zeros((vectors, width), f32)
        if expanded:
            to = target[i]
            for start in range(0, slots, STACK):
                stack = [slot_of(s) for s in range(start, min(slots, start + STACK))]
                square = dot(jnp.concatenate([source[j] for j, _ in stack], axis=0), to, NN)
                kernel = lax.rsqrt(square).astype(bf16)
                near = near + dot(jnp.concatenate([c for _, c in stack], axis=1), kernel, NN)
        else:
            for c in range(3):
                row = source[leaves + i, c : c + 1, :]
                target[c] = jnp.transpose(jnp.broadcast_to(row, (128, width)))
            for s in range(slots):
                j, charge = slot_of(s)
                halves = []
                for h in range(0, width, 128):
                    square = None
                    for c in range(3):
                        gap = target[c] - source[j, c : c + 1, h : h + 128]
                        square = gap * gap + (SOFT if square is None else square)
                    halves.append(lax.rsqrt(square).astype(bf16))
                near = near + dot(charge, jnp.concatenate(halves, axis=1), NT)
        out[:, pl.ds(pl.multiple_of(i * width, width), width)] = near
        return carry

    lax.fori_loop(0, leaves, one_leaf, 0)

    def wait_moments(d, carry):
        copy = moment_copy(d)
        copy.wait_send()
        copy.wait_recv()
        return carry

    lax.fori_loop(1, n, wait_moments, 0)

    own_group = me // group_size
    local_two = jnp.zeros((vectors, rank), f32)
    for h in range(groups):
        moment_two = moments[h * group_size][:, rank:]
        for k in range(1, group_size):
            moment_two = moment_two + moments[h * group_size + k][:, rank:]
        moment_two = moment_two * jnp.where(own_group == h, 0.0, 1.0).astype(f32)
        local_two = local_two + fine_dot(moment_two, couple_two[own_group, h], NT)
    local_one = fine_dot(local_two, cluster_transfer[0], NN)
    for s, offset in enumerate(OFFSETS):
        other = me + offset
        inside = jnp.logical_and(other >= 0, other < n)
        used = jnp.logical_and(far_list[0, s] >= 0, inside).astype(f32)
        arrived = moments[jnp.where(inside, other, me)][:, :rank] * used
        local_one = local_one + fine_dot(arrived, couple_one[0, s], NT)
    for k in range(leaves):
        local_leaf = fine_dot(local_one, leaf_transfer[k], NN).astype(bf16)
        at = slice(k * width, (k + 1) * width)
        out[:, at] = out[:, at] + dot(local_leaf, basis[k], NN)

    @pl.when(has_right)
    def _():
        for copy in halo_copies(0):
            copy.wait_send()

    @pl.when(has_left)
    def _():
        for copy in halo_copies(1):
            copy.wait_send()


def shards(
    points,
    charges,
    near_list,
    basis,
    leaf_transfer,
    cluster_transfer,
    couple_one,
    far_list,
    couple_two,
):
    n = lax.axis_size("leaf")
    leaves, rank, width = basis.shape
    vectors, panels = charges.shape
    expanded = n + 2 <= 18
    source = (3 * leaves, width, ROWS) if expanded else (3 * leaves, 8, width)
    target = (leaves, ROWS, width) if expanded else (3, width, 128)
    kind = bf16 if expanded else f32
    vmem = pl.BlockSpec(memory_space=pltpu.VMEM)
    smem = pl.BlockSpec(memory_space=pltpu.SMEM)
    return pl.pallas_call(
        functools.partial(body, n, expanded),
        out_shape=jax.ShapeDtypeStruct((vectors, panels), f32),
        in_specs=[vmem, vmem, smem, vmem, vmem, vmem, vmem, smem, vmem],
        out_specs=vmem,
        scratch_shapes=[
            pltpu.VMEM((2, *points.shape), f32),
            pltpu.VMEM((2, vectors, panels), bf16),
            pltpu.VMEM((3 * leaves, vectors, width), bf16),
            pltpu.VMEM(source, kind),
            pltpu.VMEM(target, kind),
            pltpu.VMEM((ROWS, panels), f32),
            pltpu.VMEM((n, vectors, 2 * rank), f32),
            pltpu.SemaphoreType.DMA((2, 2)),
            pltpu.SemaphoreType.DMA((2, 2)),
            pltpu.SemaphoreType.DMA((n,)),
            pltpu.SemaphoreType.DMA((n,)),
        ],
        compiler_params=pltpu.CompilerParams(
            collective_id=0, has_side_effects=True, vmem_limit_bytes=40 << 20
        ),
        name="product",
    )(
        points,
        charges,
        near_list,
        basis,
        leaf_transfer,
        cluster_transfer,
        couple_one,
        far_list,
        couple_two,
    )


def solution(mesh):
    return jax.shard_map(
        shards,
        mesh=mesh,
        in_specs=(
            P(None, ("parts", "leaf")),
            P(None, ("parts", "leaf")),
            P(("parts", "leaf"), None),
            P(("parts", "leaf"), None, None),
            P(("parts", "leaf"), None, None),
            P(("parts", "leaf"), None, None),
            P(("parts", "leaf"), None, None, None),
            P(("parts", "leaf"), None),
            P("parts", None, None, None),
        ),
        out_specs=P(None, ("parts", "leaf")),
        check_vma=False,
    )
```

```python
import functools
import math

import jax
import jax.numpy as jnp
from jax import lax
from jax.experimental import pallas as pl
from jax.experimental.pallas import tpu as pltpu
from jax.sharding import PartitionSpec as P

FAR_REACH = 4
OFFSETS = tuple(range(-FAR_REACH, -1)) + tuple(range(2, FAR_REACH + 1))
SCALE = 4.0 * math.pi
SOFT = 0.01 * SCALE * SCALE
STACK = 4
ROWS = 32
NN = (((1,), (0,)), ((), ()))
NT = (((1,), (1,)), ((), ()))
MESH = pl.DeviceIdType.MESH
f32 = jnp.float32
bf16 = jnp.bfloat16


def dot(a, b, dims):
    return lax.dot_general(a, b, dims, preferred_element_type=f32)


def fine_dot(a, b, dims):
    high = a.astype(bf16)
    low = (a - high.astype(f32)).astype(bf16)
    both = dot(jnp.concatenate([high, low], axis=0), b, dims)
    return both[: a.shape[0]] + both[a.shape[0] :]


def pieces(x):
    first = x.astype(bf16).astype(f32)
    rest = x - first
    second = rest.astype(bf16).astype(f32)
    third = (rest - second).astype(bf16).astype(f32)
    return first, second, third


def body(
    n,
    expanded,
    points_in,
    charges_in,
    near_list_in,
    basis_in,
    leaf_transfer_in,
    cluster_transfer_in,
    couple_one_in,
    far_list_in,
    couple_two_in,
    out,
    points,
    charges,
    near_list,
    basis,
    leaf_transfer,
    cluster_transfer,
    couple_one,
    far_list,
    couple_two,
    input_sem,
    halo_points,
    halo_charges,
    source_charges,
    source,
    target,
    rows,
    moments,
    halo_send,
    halo_recv,
    moment_send,
    moment_recv,
):
    leaves, rank, width = basis.shape
    vectors = charges.shape[0]
    groups = couple_two.shape[0]
    group_size = n // groups
    own_group = lax.axis_index("leaf") // group_size
    slots = near_list.shape[1]
    me = lax.axis_index("leaf")

    inputs = [
        pltpu.make_async_copy(src, dst, input_sem.at[m])
        for m, (src, dst) in enumerate(
            (
                (charges_in, charges),
                (basis_in, basis),
                (leaf_transfer_in, leaf_transfer),
                (points_in, points),
                (near_list_in, near_list),
                (cluster_transfer_in, cluster_transfer),
                (couple_one_in, couple_one),
                (far_list_in, far_list),
                (couple_two_in.at[own_group], couple_two),
            )
        )
    ]
    for copy in inputs:
        copy.start()

    barrier = pltpu.get_barrier_semaphore()

    def greet(d, carry):
        pl.semaphore_signal(
            barrier, inc=1, device_id={"leaf": lax.rem(me + d, n)}, device_id_type=MESH
        )
        return carry

    lax.fori_loop(1, n, greet, 0)

    for copy in inputs:
        copy.wait()

    moment_one = jnp.zeros((vectors, rank), f32)
    for k in range(leaves):
        own = charges[:, k * width : (k + 1) * width]
        source_charges[leaves + k] = own
        leaf_moment = dot(own, basis[k], NT)
        moment_one = moment_one + fine_dot(leaf_moment, leaf_transfer[k], NT)
    own_term = fine_dot(moment_one, cluster_transfer[0], NT)
    moments[me] = jnp.concatenate([moment_one, own_term], axis=1)

    pl.semaphore_wait(barrier, n - 1)

    def halo_copies(side):
        to = me + 1 if side == 0 else me - 1
        return [
            pltpu.make_async_remote_copy(
                src_ref=src,
                dst_ref=dst.at[side],
                send_sem=halo_send.at[side, m],
                recv_sem=halo_recv.at[side, m],
                device_id={"leaf": to},
                device_id_type=MESH,
            )
            for m, (src, dst) in enumerate(
                ((points_in, halo_points), (charges_in, halo_charges))
            )
        ]

    has_left, has_right = me > 0, me < n - 1

    @pl.when(has_right)
    def _():
        for copy in halo_copies(0):
            copy.start()

    @pl.when(has_left)
    def _():
        for copy in halo_copies(1):
            copy.start()

    def moment_copy(d):
        return pltpu.make_async_remote_copy(
            src_ref=moments.at[me],
            dst_ref=moments.at[me],
            send_sem=moment_send.at[d],
            recv_sem=moment_recv.at[d],
            device_id={"leaf": lax.rem(me + d, n)},
            device_id_type=MESH,
        )

    def send_moments(d, carry):
        moment_copy(d).start()
        return carry

    lax.fori_loop(1, n, send_moments, 0)

    @pl.when(jnp.logical_not(has_left))
    def _():
        halo_points[0] = jnp.zeros(halo_points.shape[1:], f32)
        halo_charges[0] = jnp.zeros(halo_charges.shape[1:], bf16)

    @pl.when(jnp.logical_not(has_right))
    def _():
        halo_points[1] = jnp.zeros(halo_points.shape[1:], f32)
        halo_charges[1] = jnp.zeros(halo_charges.shape[1:], bf16)

    own_points = points[...]
    if expanded:
        low = jnp.min(own_points, axis=1, keepdims=True)
        high = jnp.max(own_points, axis=1, keepdims=True)
        centre = (low + high) * 0.5
        rows[...] = jnp.zeros(rows.shape, f32)

        def put_rows(x, is_source):
            x = (x - centre) * SCALE
            square = jnp.sum(x * x, axis=0, keepdims=True)
            one = jnp.ones(square.shape, f32)
            if is_source:
                a, b, c = pieces(x)
                order = (a, a, a, b, b, c)
                ends = (*pieces(square), one, one, one)
            else:
                a, b, c = pieces(x * -2.0)
                order = (a, b, c, a, b, a)
                ends = (one, one, one, *pieces(square + SOFT))
            for m, block in enumerate(order):
                rows[3 * m : 3 * m + 3] = block
            for m, row in enumerate(ends):
                rows[18 + m : 19 + m] = row

        def put_sources(x, first):
            put_rows(x, True)
            for k in range(leaves):
                block = rows[:, k * width : (k + 1) * width]
                source[first + k] = jnp.transpose(block).astype(bf16)

        put_rows(own_points, False)
        for k in range(leaves):
            target[k] = rows[:, k * width : (k + 1) * width].astype(bf16)
    else:

        def put_sources(x, first):
            x = x * SCALE
            for k in range(leaves):
                source[first + k, 0:3] = x[:, k * width : (k + 1) * width]

    put_sources(own_points, leaves)

    @pl.when(has_left)
    def _():
        for copy in halo_copies(0):
            copy.wait_recv()

    @pl.when(has_right)
    def _():
        for copy in halo_copies(1):
            copy.wait_recv()

    for side in range(2):
        put_sources(halo_points[side], 2 * leaves * side)
        for k in range(leaves):
            source_charges[2 * leaves * side + k] = halo_charges[
                side, :, k * width : (k + 1) * width
            ]

    first_leaf = (me - 1) * leaves

    def one_leaf(i, carry):
        def slot_of(s):
            j = near_list[i, s]
            used = j >= 0
            j = jnp.clip(jnp.where(used, j - first_leaf, leaves), 0, 3 * leaves - 1)
            return j, source_charges[j] * used.astype(f32).astype(bf16)

        near = jnp.zeros((vectors, width), f32)
        if expanded:
            to = target[i]
            for start in range(0, slots, STACK):
                stack = [slot_of(s) for s in range(start, min(slots, start + STACK))]
                square = dot(jnp.concatenate([source[j] for j, _ in stack], axis=0), to, NN)
                kernel = lax.rsqrt(square).astype(bf16)
                near = near + dot(jnp.concatenate([c for _, c in stack], axis=1), kernel, NN)
        else:
            for c in range(3):
                row = source[leaves + i, c : c + 1, :]
                target[c] = jnp.transpose(jnp.broadcast_to(row, (128, width)))
            for s in range(slots):
                j, charge = slot_of(s)
                halves = []
                for h in range(0, width, 128):
                    square = None
                    for c in range(3):
                        gap = target[c] - source[j, c : c + 1, h : h + 128]
                        square = gap * gap + (SOFT if square is None else square)
                    halves.append(lax.rsqrt(square).astype(bf16))
                near = near + dot(charge, jnp.concatenate(halves, axis=1), NT)
        out[:, pl.ds(pl.multiple_of(i * width, width), width)] = near
        return carry

    lax.fori_loop(0, leaves, one_leaf, 0)

    def wait_moments(d, carry):
        copy = moment_copy(d)
        copy.wait_send()
        copy.wait_recv()
        return carry

    lax.fori_loop(1, n, wait_moments, 0)

    local_two = jnp.zeros((vectors, rank), f32)
    for h in range(groups):
        moment_two = moments[h * group_size][:, rank:]
        for k in range(1, group_size):
            moment_two = moment_two + moments[h * group_size + k][:, rank:]
        moment_two = moment_two * jnp.where(own_group == h, 0.0, 1.0).astype(f32)
        local_two = local_two + fine_dot(moment_two, couple_two[h], NT)
    local_one = fine_dot(local_two, cluster_transfer[0], NN)
    for s, offset in enumerate(OFFSETS):
        other = me + offset
        inside = jnp.logical_and(other >= 0, other < n)
        used = jnp.logical_and(far_list[0, s] >= 0, inside).astype(f32)
        arrived = moments[jnp.where(inside, other, me)][:, :rank] * used
        local_one = local_one + fine_dot(arrived, couple_one[0, s], NT)
    for k in range(leaves):
        local_leaf = fine_dot(local_one, leaf_transfer[k], NN).astype(bf16)
        at = slice(k * width, (k + 1) * width)
        out[:, at] = out[:, at] + dot(local_leaf, basis[k], NN)

    @pl.when(has_right)
    def _():
        for copy in halo_copies(0):
            copy.wait_send()

    @pl.when(has_left)
    def _():
        for copy in halo_copies(1):
            copy.wait_send()


def shards(
    points,
    charges,
    near_list,
    basis,
    leaf_transfer,
    cluster_transfer,
    couple_one,
    far_list,
    couple_two,
):
    n = lax.axis_size("leaf")
    leaves, rank, width = basis.shape
    vectors, panels = charges.shape
    expanded = n + 2 <= 18
    source = (3 * leaves, width, ROWS) if expanded else (3 * leaves, 8, width)
    target = (leaves, ROWS, width) if expanded else (3, width, 128)
    kind = bf16 if expanded else f32
    hbm = pl.BlockSpec(memory_space=pltpu.HBM)
    vmem = pl.BlockSpec(memory_space=pltpu.VMEM)
    return pl.pallas_call(
        functools.partial(body, n, expanded),
        out_shape=jax.ShapeDtypeStruct((vectors, panels), f32),
        in_specs=[hbm] * 9,
        out_specs=vmem,
        scratch_shapes=[
            pltpu.VMEM(points.shape, f32),
            pltpu.VMEM(charges.shape, bf16),
            pltpu.SMEM(near_list.shape, jnp.int32),
            pltpu.VMEM(basis.shape, bf16),
            pltpu.VMEM(leaf_transfer.shape, bf16),
            pltpu.VMEM(cluster_transfer.shape, bf16),
            pltpu.VMEM(couple_one.shape, bf16),
            pltpu.SMEM(far_list.shape, jnp.int32),
            pltpu.VMEM(couple_two.shape[1:], bf16),
            pltpu.SemaphoreType.DMA((9,)),
            pltpu.VMEM((2, *points.shape), f32),
            pltpu.VMEM((2, vectors, panels), bf16),
            pltpu.VMEM((3 * leaves, vectors, width), bf16),
            pltpu.VMEM(source, kind),
            pltpu.VMEM(target, kind),
            pltpu.VMEM((ROWS, panels), f32),
            pltpu.VMEM((n, vectors, 2 * rank), f32),
            pltpu.SemaphoreType.DMA((2, 2)),
            pltpu.SemaphoreType.DMA((2, 2)),
            pltpu.SemaphoreType.DMA((n,)),
            pltpu.SemaphoreType.DMA((n,)),
        ],
        compiler_params=pltpu.CompilerParams(
            collective_id=0, has_side_effects=True, vmem_limit_bytes=62 << 20
        ),
        name="product",
    )(
        points,
        charges,
        near_list,
        basis,
        leaf_transfer,
        cluster_transfer,
        couple_one,
        far_list,
        couple_two,
    )


def solution(mesh):
    return jax.shard_map(
        shards,
        mesh=mesh,
        in_specs=(
            P(None, ("parts", "leaf")),
            P(None, ("parts", "leaf")),
            P(("parts", "leaf"), None),
            P(("parts", "leaf"), None, None),
            P(("parts", "leaf"), None, None),
            P(("parts", "leaf"), None, None),
            P(("parts", "leaf"), None, None, None),
            P(("parts", "leaf"), None),
            P("parts", None, None, None),
        ),
        out_specs=P(None, ("parts", "leaf")),
        check_vma=False,
    )
```

```python
import functools
import math

import jax
import jax.numpy as jnp
from jax import lax
from jax.experimental import pallas as pl
from jax.experimental.pallas import tpu as pltpu
from jax.sharding import PartitionSpec as P

FAR_REACH = 4
OFFSETS = tuple(range(-FAR_REACH, -1)) + tuple(range(2, FAR_REACH + 1))
SCALE = 4.0 * math.pi
SOFT = 0.01 * SCALE * SCALE
STACK = 4
ROWS = 32
NN = (((1,), (0,)), ((), ()))
NT = (((1,), (1,)), ((), ()))
MESH = pl.DeviceIdType.MESH
f32 = jnp.float32
bf16 = jnp.bfloat16


def dot(a, b, dims):
    return lax.dot_general(a, b, dims, preferred_element_type=f32)


def fine_dot(a, b, dims):
    high = a.astype(bf16)
    low = (a - high.astype(f32)).astype(bf16)
    both = dot(jnp.concatenate([high, low], axis=0), b, dims)
    return both[: a.shape[0]] + both[a.shape[0] :]


def pieces(x):
    first = x.astype(bf16).astype(f32)
    rest = x - first
    second = rest.astype(bf16).astype(f32)
    third = (rest - second).astype(bf16).astype(f32)
    return first, second, third


def body(
    n,
    expanded,
    points_in,
    charges_in,
    near_list_in,
    basis_in,
    leaf_transfer_in,
    cluster_transfer_in,
    couple_one_in,
    far_list_in,
    couple_two_in,
    out,
    points,
    charges,
    near_list,
    basis,
    leaf_transfer,
    cluster_transfer,
    couple_one,
    far_list,
    couple_two,
    input_sem,
    halo_points,
    halo_charges,
    source_charges,
    source,
    target,
    rows,
    moments,
    halo_send,
    halo_recv,
    moment_send,
    moment_recv,
):
    leaves, rank, width = basis.shape
    vectors = charges.shape[0]
    groups = couple_two.shape[0]
    group_size = n // groups
    own_group = lax.axis_index("leaf") // group_size
    slots = near_list.shape[1]
    me = lax.axis_index("leaf")

    inputs = [
        pltpu.make_async_copy(src, dst, input_sem.at[m])
        for m, (src, dst) in enumerate(
            (
                (charges_in, charges),
                (basis_in, basis),
                (leaf_transfer_in, leaf_transfer),
                (points_in, points),
                (near_list_in, near_list),
                (cluster_transfer_in, cluster_transfer),
                (couple_one_in, couple_one),
                (far_list_in, far_list),
                (couple_two_in.at[own_group], couple_two),
            )
        )
    ]
    for copy in inputs:
        copy.start()

    barrier = pltpu.get_barrier_semaphore()

    def greet(d, carry):
        pl.semaphore_signal(
            barrier, inc=1, device_id={"leaf": lax.rem(me + d, n)}, device_id_type=MESH
        )
        return carry

    lax.fori_loop(1, n, greet, 0)

    for copy in inputs:
        copy.wait()

    moment_one = jnp.zeros((vectors, rank), f32)
    for k in range(leaves):
        own = charges[:, k * width : (k + 1) * width]
        source_charges[leaves + k] = own
        leaf_moment = dot(own, basis[k], NT)
        moment_one = moment_one + fine_dot(leaf_moment, leaf_transfer[k], NT)
    own_term = fine_dot(moment_one, cluster_transfer[0], NT)
    moments[me] = jnp.concatenate([moment_one, own_term], axis=1)

    pl.semaphore_wait(barrier, n - 1)

    def halo_copies(side):
        to = me + 1 if side == 0 else me - 1
        return [
            pltpu.make_async_remote_copy(
                src_ref=src,
                dst_ref=dst.at[side],
                send_sem=halo_send.at[side, m],
                recv_sem=halo_recv.at[side, m],
                device_id={"leaf": to},
                device_id_type=MESH,
            )
            for m, (src, dst) in enumerate(
                ((points_in, halo_points), (charges_in, halo_charges))
            )
        ]

    has_left, has_right = me > 0, me < n - 1

    @pl.when(has_right)
    def _():
        for copy in halo_copies(0):
            copy.start()

    @pl.when(has_left)
    def _():
        for copy in halo_copies(1):
            copy.start()

    def moment_copy(d):
        return pltpu.make_async_remote_copy(
            src_ref=moments.at[me],
            dst_ref=moments.at[me],
            send_sem=moment_send.at[d],
            recv_sem=moment_recv.at[d],
            device_id={"leaf": lax.rem(me + d, n)},
            device_id_type=MESH,
        )

    def send_moments(d, carry):
        moment_copy(d).start()
        return carry

    lax.fori_loop(1, n, send_moments, 0)

    @pl.when(jnp.logical_not(has_left))
    def _():
        halo_points[0] = jnp.zeros(halo_points.shape[1:], f32)
        halo_charges[0] = jnp.zeros(halo_charges.shape[1:], bf16)

    @pl.when(jnp.logical_not(has_right))
    def _():
        halo_points[1] = jnp.zeros(halo_points.shape[1:], f32)
        halo_charges[1] = jnp.zeros(halo_charges.shape[1:], bf16)

    own_points = points[...]
    if expanded:
        low = jnp.min(own_points, axis=1, keepdims=True)
        high = jnp.max(own_points, axis=1, keepdims=True)
        centre = (low + high) * 0.5
        rows[...] = jnp.zeros(rows.shape, f32)

        def put_rows(x, is_source):
            x = (x - centre) * SCALE
            square = jnp.sum(x * x, axis=0, keepdims=True)
            one = jnp.ones(square.shape, f32)
            if is_source:
                a, b, c = pieces(x)
                order = (a, a, a, b, b, c)
                ends = (*pieces(square), one, one, one)
            else:
                a, b, c = pieces(x * -2.0)
                order = (a, b, c, a, b, a)
                ends = (one, one, one, *pieces(square + SOFT))
            for m, block in enumerate(order):
                rows[3 * m : 3 * m + 3] = block
            for m, row in enumerate(ends):
                rows[18 + m : 19 + m] = row

        def put_sources(x, first):
            put_rows(x, True)
            for k in range(leaves):
                block = rows[:, k * width : (k + 1) * width]
                source[first + k] = jnp.transpose(block).astype(bf16)

        put_rows(own_points, False)
        for k in range(leaves):
            target[k] = rows[:, k * width : (k + 1) * width].astype(bf16)
    else:

        def put_sources(x, first):
            x = x * SCALE
            for k in range(leaves):
                source[first + k, 0:3] = x[:, k * width : (k + 1) * width]

    put_sources(own_points, leaves)

    @pl.when(has_left)
    def _():
        for copy in halo_copies(0):
            copy.wait_recv()

    @pl.when(has_right)
    def _():
        for copy in halo_copies(1):
            copy.wait_recv()

    for side in range(2):
        put_sources(halo_points[side], 2 * leaves * side)
        for k in range(leaves):
            source_charges[2 * leaves * side + k] = halo_charges[
                side, :, k * width : (k + 1) * width
            ]

    first_leaf = (me - 1) * leaves

    def one_leaf(i, carry):
        def slot_of(s):
            j = near_list[i, s]
            used = j >= 0
            j = jnp.clip(jnp.where(used, j - first_leaf, leaves), 0, 3 * leaves - 1)
            return j, source_charges[j] * used.astype(f32).astype(bf16)

        near = jnp.zeros((vectors, width), f32)
        if expanded:
            to = target[i]
            for start in range(0, slots, STACK):
                stack = [slot_of(s) for s in range(start, min(slots, start + STACK))]
                square = dot(jnp.concatenate([source[j] for j, _ in stack], axis=0), to, NN)
                kernel = lax.rsqrt(square).astype(bf16)
                near = near + dot(jnp.concatenate([c for _, c in stack], axis=1), kernel, NN)
        else:
            for c in range(3):
                row = source[leaves + i, c : c + 1, :]
                target[c] = jnp.transpose(jnp.broadcast_to(row, (128, width)))
            for s in range(slots):
                j, charge = slot_of(s)
                halves = []
                for h in range(0, width, 128):
                    square = None
                    for c in range(3):
                        gap = target[c] - source[j, c : c + 1, h : h + 128]
                        square = gap * gap + (SOFT if square is None else square)
                    halves.append(lax.rsqrt(square).astype(bf16))
                near = near + dot(charge, jnp.concatenate(halves, axis=1), NT)
        out[:, pl.ds(pl.multiple_of(i * width, width), width)] = near
        return carry

    lax.fori_loop(0, leaves, one_leaf, 0)

    def wait_moments(d, carry):
        copy = moment_copy(d)
        copy.wait_send()
        copy.wait_recv()
        return carry

    lax.fori_loop(1, n, wait_moments, 0)

    local_two = jnp.zeros((vectors, rank), f32)
    for h in range(groups):
        moment_two = moments[h * group_size][:, rank:]
        for k in range(1, group_size):
            moment_two = moment_two + moments[h * group_size + k][:, rank:]
        moment_two = moment_two * jnp.where(own_group == h, 0.0, 1.0).astype(f32)
        local_two = local_two + fine_dot(moment_two, couple_two[h], NT)
    local_one = fine_dot(local_two, cluster_transfer[0], NN)
    for s, offset in enumerate(OFFSETS):
        other = me + offset
        inside = jnp.logical_and(other >= 0, other < n)
        used = jnp.logical_and(far_list[0, s] >= 0, inside).astype(f32)
        arrived = moments[jnp.where(inside, other, me)][:, :rank] * used
        local_one = local_one + fine_dot(arrived, couple_one[0, s], NT)
    for k in range(leaves):
        local_leaf = fine_dot(local_one, leaf_transfer[k], NN).astype(bf16)
        at = slice(k * width, (k + 1) * width)
        out[:, at] = out[:, at] + dot(local_leaf, basis[k], NN)

    @pl.when(has_right)
    def _():
        for copy in halo_copies(0):
            copy.wait_send()

    @pl.when(has_left)
    def _():
        for copy in halo_copies(1):
            copy.wait_send()


def shards(
    points,
    charges,
    near_list,
    basis,
    leaf_transfer,
    cluster_transfer,
    couple_one,
    far_list,
    couple_two,
):
    n = lax.axis_size("leaf")
    leaves, rank, width = basis.shape
    vectors, panels = charges.shape
    expanded = n + 2 <= 18
    source = (3 * leaves, width, ROWS) if expanded else (3 * leaves, 8, width)
    target = (leaves, ROWS, width) if expanded else (3, width, 128)
    kind = bf16 if expanded else f32
    hbm = pl.BlockSpec(memory_space=pltpu.HBM)
    vmem = pl.BlockSpec(memory_space=pltpu.VMEM)
    return pl.pallas_call(
        functools.partial(body, n, expanded),
        out_shape=pltpu.VMEM((vectors, panels), f32),
        in_specs=[hbm] * 9,
        out_specs=vmem,
        scratch_shapes=[
            pltpu.VMEM(points.shape, f32),
            pltpu.VMEM(charges.shape, bf16),
            pltpu.SMEM(near_list.shape, jnp.int32),
            pltpu.VMEM(basis.shape, bf16),
            pltpu.VMEM(leaf_transfer.shape, bf16),
            pltpu.VMEM(cluster_transfer.shape, bf16),
            pltpu.VMEM(couple_one.shape, bf16),
            pltpu.SMEM(far_list.shape, jnp.int32),
            pltpu.VMEM(couple_two.shape[1:], bf16),
            pltpu.SemaphoreType.DMA((9,)),
            pltpu.VMEM((2, *points.shape), f32),
            pltpu.VMEM((2, vectors, panels), bf16),
            pltpu.VMEM((3 * leaves, vectors, width), bf16),
            pltpu.VMEM(source, kind),
            pltpu.VMEM(target, kind),
            pltpu.VMEM((ROWS, panels), f32),
            pltpu.VMEM((n, vectors, 2 * rank), f32),
            pltpu.SemaphoreType.DMA((2, 2)),
            pltpu.SemaphoreType.DMA((2, 2)),
            pltpu.SemaphoreType.DMA((n,)),
            pltpu.SemaphoreType.DMA((n,)),
        ],
        compiler_params=pltpu.CompilerParams(
            collective_id=0, has_side_effects=True, vmem_limit_bytes=62 << 20
        ),
        name="product",
    )(
        points,
        charges,
        near_list,
        basis,
        leaf_transfer,
        cluster_transfer,
        couple_one,
        far_list,
        couple_two,
    )


def solution(mesh):
    return jax.shard_map(
        shards,
        mesh=mesh,
        in_specs=(
            P(None, ("parts", "leaf")),
            P(None, ("parts", "leaf")),
            P(("parts", "leaf"), None),
            P(("parts", "leaf"), None, None),
            P(("parts", "leaf"), None, None),
            P(("parts", "leaf"), None, None),
            P(("parts", "leaf"), None, None, None),
            P(("parts", "leaf"), None),
            P("parts", None, None, None),
        ),
        out_specs=P(None, ("parts", "leaf")),
        check_vma=False,
    )
```

```python
import functools
import math

import jax
import jax.numpy as jnp
from jax import lax
from jax.experimental import pallas as pl
from jax.experimental.pallas import tpu as pltpu
from jax.sharding import PartitionSpec as P

FAR_REACH = 4
OFFSETS = tuple(range(-FAR_REACH, -1)) + tuple(range(2, FAR_REACH + 1))
SCALE = 4.0 * math.pi
SOFT = 0.01 * SCALE * SCALE
STACK = 4
ROWS = 32
UNROLL = 5
LAST = 4
NN = (((1,), (0,)), ((), ()))
NT = (((1,), (1,)), ((), ()))
MESH = pl.DeviceIdType.MESH
f32 = jnp.float32
bf16 = jnp.bfloat16


def dot(a, b, dims):
    return lax.dot_general(a, b, dims, preferred_element_type=f32)


def fine_dot(a, b, dims):
    high = a.astype(bf16)
    low = (a - high.astype(f32)).astype(bf16)
    both = dot(jnp.concatenate([high, low], axis=0), b, dims)
    return both[: a.shape[0]] + both[a.shape[0] :]


def pieces(x):
    first = x.astype(bf16).astype(f32)
    rest = x - first
    second = rest.astype(bf16).astype(f32)
    third = (rest - second).astype(bf16).astype(f32)
    return first, second, third


def body(
    n,
    expanded,
    points_in,
    charges_in,
    near_list_in,
    basis_in,
    leaf_transfer_in,
    cluster_transfer_in,
    couple_one_in,
    far_list_in,
    couple_two_in,
    out,
    points,
    charges,
    near_list,
    basis,
    leaf_transfer,
    cluster_transfer,
    couple_one,
    far_list,
    couple_two,
    input_sem,
    halo_points,
    halo_charges,
    source_charges,
    source,
    target,
    rows,
    moments,
    halo_send,
    halo_recv,
    moment_send,
    moment_recv,
    news,
):
    leaves, rank, width = basis.shape
    vectors = charges.shape[0]
    groups = couple_two.shape[0]
    group_size = n // groups
    own_group = lax.axis_index("leaf") // group_size
    slots = near_list.shape[1]
    me = lax.axis_index("leaf")

    barrier = pltpu.get_barrier_semaphore()

    has_left, has_right = me > 0, me < n - 1

    def on_line(step, act_left, act_right):
        pl.when(me >= step)(functools.partial(act_left, {"leaf": me - step}))
        pl.when(me < n - step)(functools.partial(act_right, {"leaf": me + step}))

    def greet(device):
        pl.semaphore_signal(barrier, inc=1, device_id=device, device_id_type=MESH)

    on_line(1, greet, greet)

    rounds = max(1, (n - 2).bit_length())

    def announce(r):
        def to(side):
            return lambda device: pl.semaphore_signal(
                news.at[r, side], inc=1, device_id=device, device_id_type=MESH
            )

        on_line(2**r, to(1), to(0))

    def hear(r):
        def of(side):
            return lambda device: pl.semaphore_wait(news.at[r, side], 1)

        on_line(2**r, of(0), of(1))
        if r + 1 < rounds:
            announce(r + 1)

    inputs = [
        pltpu.make_async_copy(src, dst, input_sem.at[m])
        for m, (src, dst) in enumerate(
            (
                (charges_in, charges),
                (basis_in, basis),
                (leaf_transfer_in, leaf_transfer),
                (cluster_transfer_in, cluster_transfer),
                (points_in, points),
                (near_list_in, near_list),
                (couple_one_in, couple_one),
                (far_list_in, far_list),
                (couple_two_in.at[own_group], couple_two),
            )
        )
    ]
    for copy in inputs:
        copy.start()

    pl.semaphore_wait(barrier, has_left.astype(jnp.int32) + has_right.astype(jnp.int32))
    announce(0)

    def halo_copies(side):
        to = me + 1 if side == 0 else me - 1
        return [
            pltpu.make_async_remote_copy(
                src_ref=src,
                dst_ref=dst.at[side],
                send_sem=halo_send.at[side, m],
                recv_sem=halo_recv.at[side, m],
                device_id={"leaf": to},
                device_id_type=MESH,
            )
            for m, (src, dst) in enumerate(
                ((points_in, halo_points), (charges_in, halo_charges))
            )
        ]

    @pl.when(has_right)
    def _():
        for copy in halo_copies(0):
            copy.start()

    @pl.when(has_left)
    def _():
        for copy in halo_copies(1):
            copy.start()

    for copy in inputs[:4]:
        copy.wait()

    moment_one = jnp.zeros((vectors, rank), f32)
    for k in range(leaves):
        own = charges[:, k * width : (k + 1) * width]
        source_charges[leaves + k] = own
        leaf_moment = dot(own, basis[k], NT)
        moment_one = moment_one + fine_dot(leaf_moment, leaf_transfer[k], NT)
    own_term = fine_dot(moment_one, cluster_transfer[0], NT)
    moments[me] = jnp.concatenate([moment_one, own_term], axis=1)

    def moment_copy(d):
        return pltpu.make_async_remote_copy(
            src_ref=moments.at[me],
            dst_ref=moments.at[me],
            send_sem=moment_send,
            recv_sem=moment_recv,
            device_id={"leaf": lax.rem(me + d, n)},
            device_id_type=MESH,
        )

    def send_moments(d, carry):
        moment_copy(d).start()
        return carry


    @pl.when(jnp.logical_not(has_left))
    def _():
        halo_points[0] = jnp.zeros(halo_points.shape[1:], f32)
        halo_charges[0] = jnp.zeros(halo_charges.shape[1:], bf16)

    @pl.when(jnp.logical_not(has_right))
    def _():
        halo_points[1] = jnp.zeros(halo_points.shape[1:], f32)
        halo_charges[1] = jnp.zeros(halo_charges.shape[1:], bf16)

    inputs[4].wait()
    own_points = points[...]
    if expanded:
        low = jnp.min(own_points, axis=1, keepdims=True)
        high = jnp.max(own_points, axis=1, keepdims=True)
        centre = (low + high) * 0.5
        rows[...] = jnp.zeros(rows.shape, f32)

        def put_rows(x, is_source):
            x = (x - centre) * SCALE
            square = jnp.sum(x * x, axis=0, keepdims=True)
            one = jnp.ones(square.shape, f32)
            if is_source:
                a, b, c = pieces(x)
                order = (a, a, a, b, b, c)
                ends = (*pieces(square), one, one, one)
            else:
                a, b, c = pieces(x * -2.0)
                order = (a, b, c, a, b, a)
                ends = (one, one, one, *pieces(square + SOFT))
            for m, block in enumerate(order):
                rows[3 * m : 3 * m + 3] = block
            for m, row in enumerate(ends):
                rows[18 + m : 19 + m] = row

        def put_sources(x, first):
            put_rows(x, True)
            for k in range(leaves):
                block = rows[:, k * width : (k + 1) * width]
                source[first + k] = jnp.transpose(block).astype(bf16)

        put_rows(own_points, False)
        for k in range(leaves):
            target[k] = rows[:, k * width : (k + 1) * width].astype(bf16)
    else:

        def put_sources(x, first):
            x = x * SCALE
            for k in range(leaves):
                source[first + k, 0:3] = x[:, k * width : (k + 1) * width]

    put_sources(own_points, leaves)

    @pl.when(has_left)
    def _():
        for copy in halo_copies(0):
            copy.wait_recv()

    @pl.when(has_right)
    def _():
        for copy in halo_copies(1):
            copy.wait_recv()

    for side in range(2):
        put_sources(halo_points[side], 2 * leaves * side)
        for k in range(leaves):
            source_charges[2 * leaves * side + k] = halo_charges[
                side, :, k * width : (k + 1) * width
            ]

    for copy in inputs[5:]:
        copy.wait()
    first_leaf = (me - 1) * leaves

    def one_leaf(i, carry):
        def slot_of(s):
            j = near_list[i, s]
            used = j >= 0
            j = jnp.clip(jnp.where(used, j - first_leaf, leaves), 0, 3 * leaves - 1)
            return j, source_charges[j] * used.astype(f32).astype(bf16)

        near = jnp.zeros((vectors, width), f32)
        if expanded:
            to = target[i]
            for start in range(0, slots, STACK):
                stack = [slot_of(s) for s in range(start, min(slots, start + STACK))]
                square = dot(jnp.concatenate([source[j] for j, _ in stack], axis=0), to, NN)
                kernel = lax.rsqrt(square).astype(bf16)
                near = near + dot(jnp.concatenate([c for _, c in stack], axis=1), kernel, NN)
        else:
            for c in range(3):
                row = source[leaves + i, c : c + 1, :]
                target[c] = jnp.transpose(jnp.broadcast_to(row, (128, width)))
            for s in range(slots):
                j, charge = slot_of(s)
                halves = []
                for h in range(0, width, 128):
                    square = None
                    for c in range(3):
                        gap = target[c] - source[j, c : c + 1, h : h + 128]
                        square = gap * gap + (SOFT if square is None else square)
                    halves.append(lax.rsqrt(square).astype(bf16))
                near = near + dot(charge, jnp.concatenate(halves, axis=1), NT)
        out[:, pl.ds(pl.multiple_of(i * width, width), width)] = near
        return carry

    done = 0
    for r in range(rounds):
        upto = r * (leaves - LAST) // max(1, rounds - 1)
        if upto > done:
            lax.fori_loop(done, upto, one_leaf, 0)
        done = upto
        hear(r)
    lax.fori_loop(1, n, send_moments, 0, unroll=UNROLL)
    lax.fori_loop(done, leaves, one_leaf, 0)

    others = moments.at[pl.ds(0, n - 1)]
    pltpu.make_async_copy(others, others, moment_recv).wait()

    local_two = jnp.zeros((vectors, rank), f32)
    for h in range(groups):
        moment_two = moments[h * group_size][:, rank:]
        for k in range(1, group_size):
            moment_two = moment_two + moments[h * group_size + k][:, rank:]
        moment_two = moment_two * jnp.where(own_group == h, 0.0, 1.0).astype(f32)
        local_two = local_two + fine_dot(moment_two, couple_two[h], NT)
    local_one = fine_dot(local_two, cluster_transfer[0], NN)
    for s, offset in enumerate(OFFSETS):
        other = me + offset
        inside = jnp.logical_and(other >= 0, other < n)
        used = jnp.logical_and(far_list[0, s] >= 0, inside).astype(f32)
        arrived = moments[jnp.where(inside, other, me)][:, :rank] * used
        local_one = local_one + fine_dot(arrived, couple_one[0, s], NT)
    for k in range(leaves):
        local_leaf = fine_dot(local_one, leaf_transfer[k], NN).astype(bf16)
        at = slice(k * width, (k + 1) * width)
        out[:, at] = out[:, at] + dot(local_leaf, basis[k], NN)

    pltpu.make_async_copy(others, others, moment_send).wait()

    @pl.when(has_right)
    def _():
        for copy in halo_copies(0):
            copy.wait_send()

    @pl.when(has_left)
    def _():
        for copy in halo_copies(1):
            copy.wait_send()


def shards(
    points,
    charges,
    near_list,
    basis,
    leaf_transfer,
    cluster_transfer,
    couple_one,
    far_list,
    couple_two,
):
    n = lax.axis_size("leaf")
    leaves, rank, width = basis.shape
    vectors, panels = charges.shape
    expanded = n + 2 <= 18
    source = (3 * leaves, width, ROWS) if expanded else (3 * leaves, 8, width)
    target = (leaves, ROWS, width) if expanded else (3, width, 128)
    kind = bf16 if expanded else f32
    hbm = pl.BlockSpec(memory_space=pltpu.HBM)
    vmem = pl.BlockSpec(memory_space=pltpu.VMEM)
    return pl.pallas_call(
        functools.partial(body, n, expanded),
        out_shape=pltpu.VMEM((vectors, panels), f32),
        in_specs=[hbm] * 9,
        out_specs=vmem,
        scratch_shapes=[
            pltpu.VMEM(points.shape, f32),
            pltpu.VMEM(charges.shape, bf16),
            pltpu.SMEM(near_list.shape, jnp.int32),
            pltpu.VMEM(basis.shape, bf16),
            pltpu.VMEM(leaf_transfer.shape, bf16),
            pltpu.VMEM(cluster_transfer.shape, bf16),
            pltpu.VMEM(couple_one.shape, bf16),
            pltpu.SMEM(far_list.shape, jnp.int32),
            pltpu.VMEM(couple_two.shape[1:], bf16),
            pltpu.SemaphoreType.DMA((9,)),
            pltpu.VMEM((2, *points.shape), f32),
            pltpu.VMEM((2, vectors, panels), bf16),
            pltpu.VMEM((3 * leaves, vectors, width), bf16),
            pltpu.VMEM(source, kind),
            pltpu.VMEM(target, kind),
            pltpu.VMEM((ROWS, panels), f32),
            pltpu.VMEM((n, vectors, 2 * rank), f32),
            pltpu.SemaphoreType.DMA((2, 2)),
            pltpu.SemaphoreType.DMA((2, 2)),
            pltpu.SemaphoreType.DMA,
            pltpu.SemaphoreType.DMA,
            pltpu.SemaphoreType.REGULAR(((n - 1).bit_length(), 2)),
        ],
        compiler_params=pltpu.CompilerParams(
            collective_id=0, has_side_effects=True, vmem_limit_bytes=62 << 20
        ),
        name="product",
    )(
        points,
        charges,
        near_list,
        basis,
        leaf_transfer,
        cluster_transfer,
        couple_one,
        far_list,
        couple_two,
    )


def solution(mesh):
    return jax.shard_map(
        shards,
        mesh=mesh,
        in_specs=(
            P(None, ("parts", "leaf")),
            P(None, ("parts", "leaf")),
            P(("parts", "leaf"), None),
            P(("parts", "leaf"), None, None),
            P(("parts", "leaf"), None, None),
            P(("parts", "leaf"), None, None),
            P(("parts", "leaf"), None, None, None),
            P(("parts", "leaf"), None),
            P("parts", None, None, None),
        ),
        out_specs=P(None, ("parts", "leaf")),
        check_vma=False,
    )
```

```python
import functools
import math

import jax
import jax.numpy as jnp
from jax import lax
from jax.experimental import pallas as pl
from jax.experimental.pallas import tpu as pltpu
from jax.sharding import PartitionSpec as P

FAR_REACH = 4
OFFSETS = tuple(range(-FAR_REACH, -1)) + tuple(range(2, FAR_REACH + 1))
SCALE = 4.0 * math.pi
SOFT = 0.01 * SCALE * SCALE
STACK = 4
ROWS = 32
UNROLL = 5
LAST = 4
NN = (((1,), (0,)), ((), ()))
NT = (((1,), (1,)), ((), ()))
MESH = pl.DeviceIdType.MESH
f32 = jnp.float32
bf16 = jnp.bfloat16


def dot(a, b, dims):
    return lax.dot_general(a, b, dims, preferred_element_type=f32)


def fine_dot(a, b, dims):
    high = a.astype(bf16)
    low = (a - high.astype(f32)).astype(bf16)
    both = dot(jnp.concatenate([high, low], axis=0), b, dims)
    return both[: a.shape[0]] + both[a.shape[0] :]


def pieces(x):
    first = x.astype(bf16).astype(f32)
    rest = x - first
    second = rest.astype(bf16).astype(f32)
    third = (rest - second).astype(bf16).astype(f32)
    return first, second, third


def body(
    n,
    expanded,
    points_in,
    charges_in,
    near_list_in,
    basis_in,
    leaf_transfer_in,
    cluster_transfer_in,
    couple_one_in,
    far_list_in,
    couple_two_in,
    out,
    points,
    charges,
    near_list,
    basis,
    leaf_transfer,
    cluster_transfer,
    couple_one,
    far_list,
    couple_two,
    input_sem,
    halo_points,
    halo_charges,
    source_charges,
    source,
    target,
    rows,
    moments,
    halo_send,
    halo_recv,
    moment_send,
    moment_recv,
    news,
):
    leaves, rank, width = basis.shape
    vectors = charges.shape[0]
    groups = couple_two.shape[0]
    group_size = n // groups
    own_group = lax.axis_index("leaf") // group_size
    slots = near_list.shape[1]
    me = lax.axis_index("leaf")

    barrier = pltpu.get_barrier_semaphore()

    has_left, has_right = me > 0, me < n - 1

    def on_line(step, act_left, act_right):
        pl.when(me >= step)(functools.partial(act_left, {"leaf": me - step}))
        pl.when(me < n - step)(functools.partial(act_right, {"leaf": me + step}))

    def greet(device):
        pl.semaphore_signal(barrier, inc=1, device_id=device, device_id_type=MESH)

    on_line(1, greet, greet)

    rounds = max(1, (n - 2).bit_length())

    def announce(r):
        def to(side):
            return lambda device: pl.semaphore_signal(
                news.at[r, side], inc=1, device_id=device, device_id_type=MESH
            )

        on_line(2**r, to(1), to(0))

    def hear(r):
        def of(side):
            return lambda device: pl.semaphore_wait(news.at[r, side], 1)

        on_line(2**r, of(0), of(1))
        if r + 1 < rounds:
            announce(r + 1)

    inputs = [
        pltpu.make_async_copy(src, dst, input_sem.at[m])
        for m, (src, dst) in enumerate(
            (
                (charges_in, charges),
                (basis_in, basis),
                (leaf_transfer_in, leaf_transfer),
                (cluster_transfer_in, cluster_transfer),
                (points_in, points),
                (near_list_in, near_list),
                (couple_one_in, couple_one),
                (far_list_in, far_list),
                (couple_two_in.at[own_group], couple_two),
            )
        )
    ]
    for copy in inputs:
        copy.start()

    pl.semaphore_wait(barrier, has_left.astype(jnp.int32) + has_right.astype(jnp.int32))
    announce(0)

    def halo_copies(side):
        to = me + 1 if side == 0 else me - 1
        return [
            pltpu.make_async_remote_copy(
                src_ref=src,
                dst_ref=dst.at[side],
                send_sem=halo_send.at[side, m],
                recv_sem=halo_recv.at[side, m],
                device_id={"leaf": to},
                device_id_type=MESH,
            )
            for m, (src, dst) in enumerate(
                ((points_in, halo_points), (charges_in, halo_charges))
            )
        ]

    @pl.when(has_right)
    def _():
        for copy in halo_copies(0):
            copy.start()

    @pl.when(has_left)
    def _():
        for copy in halo_copies(1):
            copy.start()

    for copy in inputs[:4]:
        copy.wait()

    moment_one = jnp.zeros((vectors, rank), f32)
    for k in range(leaves):
        own = charges[:, k * width : (k + 1) * width]
        source_charges[leaves + k] = own
        leaf_moment = dot(own, basis[k], NT)
        moment_one = moment_one + fine_dot(leaf_moment, leaf_transfer[k], NT)
    own_term = fine_dot(moment_one, cluster_transfer[0], NT)
    moments[me] = jnp.concatenate([moment_one, own_term], axis=1)

    def moment_copy(d):
        return pltpu.make_async_remote_copy(
            src_ref=moments.at[me],
            dst_ref=moments.at[me],
            send_sem=moment_send,
            recv_sem=moment_recv,
            device_id={"leaf": lax.rem(me + d, n)},
            device_id_type=MESH,
        )

    def send_moments(d, carry):
        moment_copy(d).start()
        return carry


    @pl.when(jnp.logical_not(has_left))
    def _():
        halo_points[0] = jnp.zeros(halo_points.shape[1:], f32)
        halo_charges[0] = jnp.zeros(halo_charges.shape[1:], bf16)

    @pl.when(jnp.logical_not(has_right))
    def _():
        halo_points[1] = jnp.zeros(halo_points.shape[1:], f32)
        halo_charges[1] = jnp.zeros(halo_charges.shape[1:], bf16)

    inputs[4].wait()
    own_points = points[...]
    if expanded:
        low = jnp.min(own_points, axis=1, keepdims=True)
        high = jnp.max(own_points, axis=1, keepdims=True)
        centre = (low + high) * 0.5
        rows[...] = jnp.zeros(rows.shape, f32)

        def put_rows(x, is_source):
            x = (x - centre) * SCALE
            square = jnp.sum(x * x, axis=0, keepdims=True)
            one = jnp.ones(square.shape, f32)
            if is_source:
                a, b, c = pieces(x)
                order = (a, a, a, b, b, c)
                ends = (*pieces(square), one, one, one)
            else:
                a, b, c = pieces(x * -2.0)
                order = (a, b, c, a, b, a)
                ends = (one, one, one, *pieces(square + SOFT))
            for m, block in enumerate(order):
                rows[3 * m : 3 * m + 3] = block
            for m, row in enumerate(ends):
                rows[18 + m : 19 + m] = row

        def put_sources(x, first):
            put_rows(x, True)
            for k in range(leaves):
                block = rows[:, k * width : (k + 1) * width]
                source[first + k] = jnp.transpose(block).astype(bf16)

        put_rows(own_points, False)
        for k in range(leaves):
            target[k] = rows[:, k * width : (k + 1) * width].astype(bf16)
    else:

        def put_sources(x, first):
            x = x * SCALE
            for k in range(leaves):
                source[first + k, 0:3] = x[:, k * width : (k + 1) * width]

    put_sources(own_points, leaves)

    @pl.when(has_left)
    def _():
        for copy in halo_copies(0):
            copy.wait_recv()

    @pl.when(has_right)
    def _():
        for copy in halo_copies(1):
            copy.wait_recv()

    for side in range(2):
        put_sources(halo_points[side], 2 * leaves * side)
        for k in range(leaves):
            source_charges[2 * leaves * side + k] = halo_charges[
                side, :, k * width : (k + 1) * width
            ]

    for copy in inputs[5:]:
        copy.wait()
    first_leaf = (me - 1) * leaves

    def one_leaf(i, carry):
        def slot_of(s):
            j = near_list[i, s]
            used = j >= 0
            j = jnp.clip(jnp.where(used, j - first_leaf, leaves), 0, 3 * leaves - 1)
            return j, source_charges[j] * used.astype(f32).astype(bf16)

        near = jnp.zeros((vectors, width), f32)
        if expanded:
            to = target[i]
            for start in range(0, slots, STACK):
                stack = [slot_of(s) for s in range(start, min(slots, start + STACK))]
                square = dot(jnp.concatenate([source[j] for j, _ in stack], axis=0), to, NN)
                kernel = lax.rsqrt(square).astype(bf16)
                near = near + dot(jnp.concatenate([c for _, c in stack], axis=1), kernel, NN)
        else:
            for c in range(3):
                row = source[leaves + i, c : c + 1, :]
                target[c] = jnp.transpose(jnp.broadcast_to(row, (128, width)))
            for s in range(slots):
                j, charge = slot_of(s)
                halves = []
                for h in range(0, width, 128):
                    square = None
                    for c in range(3):
                        gap = target[c] - source[j, c : c + 1, h : h + 128]
                        square = gap * gap + (SOFT if square is None else square)
                    halves.append(lax.rsqrt(square).astype(bf16))
                near = near + dot(charge, jnp.concatenate(halves, axis=1), NT)
        out[:, pl.ds(pl.multiple_of(i * width, width), width)] = near
        return carry

    done = 0
    for r in range(rounds):
        upto = r * (leaves - LAST) // max(1, rounds - 1)
        if upto > done:
            lax.fori_loop(done, upto, one_leaf, 0, unroll=min(2, upto - done))
        done = upto
        hear(r)
    lax.fori_loop(1, n, send_moments, 0, unroll=UNROLL)
    lax.fori_loop(done, leaves, one_leaf, 0, unroll=2)

    others = moments.at[pl.ds(0, n - 1)]
    pltpu.make_async_copy(others, others, moment_recv).wait()

    local_two = jnp.zeros((vectors, rank), f32)
    for h in range(groups):
        moment_two = moments[h * group_size][:, rank:]
        for k in range(1, group_size):
            moment_two = moment_two + moments[h * group_size + k][:, rank:]
        moment_two = moment_two * jnp.where(own_group == h, 0.0, 1.0).astype(f32)
        local_two = local_two + fine_dot(moment_two, couple_two[h], NT)
    local_one = fine_dot(local_two, cluster_transfer[0], NN)
    for s, offset in enumerate(OFFSETS):
        other = me + offset
        inside = jnp.logical_and(other >= 0, other < n)
        used = jnp.logical_and(far_list[0, s] >= 0, inside).astype(f32)
        arrived = moments[jnp.where(inside, other, me)][:, :rank] * used
        local_one = local_one + fine_dot(arrived, couple_one[0, s], NT)
    for k in range(leaves):
        local_leaf = fine_dot(local_one, leaf_transfer[k], NN).astype(bf16)
        at = slice(k * width, (k + 1) * width)
        out[:, at] = out[:, at] + dot(local_leaf, basis[k], NN)

    pltpu.make_async_copy(others, others, moment_send).wait()

    @pl.when(has_right)
    def _():
        for copy in halo_copies(0):
            copy.wait_send()

    @pl.when(has_left)
    def _():
        for copy in halo_copies(1):
            copy.wait_send()


def shards(
    points,
    charges,
    near_list,
    basis,
    leaf_transfer,
    cluster_transfer,
    couple_one,
    far_list,
    couple_two,
):
    n = lax.axis_size("leaf")
    leaves, rank, width = basis.shape
    vectors, panels = charges.shape
    expanded = n + 2 <= 18
    source = (3 * leaves, width, ROWS) if expanded else (3 * leaves, 8, width)
    target = (leaves, ROWS, width) if expanded else (3, width, 128)
    kind = bf16 if expanded else f32
    hbm = pl.BlockSpec(memory_space=pltpu.HBM)
    vmem = pl.BlockSpec(memory_space=pltpu.VMEM)
    return pl.pallas_call(
        functools.partial(body, n, expanded),
        out_shape=pltpu.VMEM((vectors, panels), f32),
        in_specs=[hbm] * 9,
        out_specs=vmem,
        scratch_shapes=[
            pltpu.VMEM(points.shape, f32),
            pltpu.VMEM(charges.shape, bf16),
            pltpu.SMEM(near_list.shape, jnp.int32),
            pltpu.VMEM(basis.shape, bf16),
            pltpu.VMEM(leaf_transfer.shape, bf16),
            pltpu.VMEM(cluster_transfer.shape, bf16),
            pltpu.VMEM(couple_one.shape, bf16),
            pltpu.SMEM(far_list.shape, jnp.int32),
            pltpu.VMEM(couple_two.shape[1:], bf16),
            pltpu.SemaphoreType.DMA((9,)),
            pltpu.VMEM((2, *points.shape), f32),
            pltpu.VMEM((2, vectors, panels), bf16),
            pltpu.VMEM((3 * leaves, vectors, width), bf16),
            pltpu.VMEM(source, kind),
            pltpu.VMEM(target, kind),
            pltpu.VMEM((ROWS, panels), f32),
            pltpu.VMEM((n, vectors, 2 * rank), f32),
            pltpu.SemaphoreType.DMA((2, 2)),
            pltpu.SemaphoreType.DMA((2, 2)),
            pltpu.SemaphoreType.DMA,
            pltpu.SemaphoreType.DMA,
            pltpu.SemaphoreType.REGULAR(((n - 1).bit_length(), 2)),
        ],
        compiler_params=pltpu.CompilerParams(
            collective_id=0, has_side_effects=True, vmem_limit_bytes=62 << 20
        ),
        name="product",
    )(
        points,
        charges,
        near_list,
        basis,
        leaf_transfer,
        cluster_transfer,
        couple_one,
        far_list,
        couple_two,
    )


def solution(mesh):
    return jax.shard_map(
        shards,
        mesh=mesh,
        in_specs=(
            P(None, ("parts", "leaf")),
            P(None, ("parts", "leaf")),
            P(("parts", "leaf"), None),
            P(("parts", "leaf"), None, None),
            P(("parts", "leaf"), None, None),
            P(("parts", "leaf"), None, None),
            P(("parts", "leaf"), None, None, None),
            P(("parts", "leaf"), None),
            P("parts", None, None, None),
        ),
        out_specs=P(None, ("parts", "leaf")),
        check_vma=False,
    )
```
